256 devices in a mesh: lon: 16 (over y, x_lo, core), lat: 16 (over z, x_hi).
Axes of the slice: x: 4 (x_hi: 2, x_lo: 2; x = x_hi * 2 + x_lo), y: 4, z: 8, core: 2. Of those that a mesh axis runs over, the one named last changes fastest.
Arguments:
- levels_in: bfloat16 [13, 96, 192, 512], P(None, 'lat', 'lon'), may hold values from -6 to 6
- surface: bfloat16 [96, 192, 512], P('lat', 'lon'), may hold values from -6 to 6
- latents: bfloat16 [3, 512], replicated, may hold values from -3 to 3
- level_codes: bfloat16 [13, 512], replicated, may hold values from -3 to 3
- norm_gains: float32 [6, 512], replicated, may hold values from 0.1 to 1.9
- agg_query_w: bfloat16 [512, 512], P('lat'), may hold values from -0.25 to 0.25
- agg_key_w: bfloat16 [512, 512], P('lat'), may hold values from -0.25 to 0.25
- agg_value_w: bfloat16 [512, 512], P('lat'), may hold values from -0.25 to 0.25
- agg_out_w: bfloat16 [512, 512], P('lat'), may hold values from -0.25 to 0.25
- dec_query_w: bfloat16 [512, 512], P('lat'), may hold values from -0.25 to 0.25
- dec_key_w: bfloat16 [512, 512], P('lat'), may hold values from -0.25 to 0.25
- dec_value_w: bfloat16 [512, 512], P('lat'), may hold values from -0.25 to 0.25
- dec_out_w: bfloat16 [512, 512], P('lat'), may hold values from -0.25 to 0.25
- qkv_w: bfloat16 [2, 512, 1536], P(None, 'lat'), may hold values from -0.25 to 0.25
- proj_w: bfloat16 [2, 512, 512], P(None, 'lat'), may hold values from -0.25 to 0.25
- mlp_in: bfloat16 [2, 2048, 512], P(None, 'lat'), may hold values from -0.25 to 0.25
- mlp_out: bfloat16 [2, 2048, 512], P(None, 'lat'), may hold values from -0.125 to 0.125
- regions: int32 [4, 96], P(None, 'lat'), may hold values from 0 to 2
Outputs:
- decoded: bfloat16 [13, 96, 192, 512], P(None, 'lat', 'lon')
The draws below stay inside these ranges and needn't reach their ends.
All inputs are finite; a program needn't handle non-finite values.
Results may differ from the reference program's by a relative error of at most 0.025.
Values may be sent and summed in bfloat16 or wider, within the bound.
A program may use at most 64 MiB of HBM per device.

```python
import jax
import jax.numpy as jnp
from jax import lax

D = 512
HEADS = 16
HD = 32
FF = 2048
LEVELS = 13
LATENT = 3
ZL = 4
WZ = 2
WLAT = 6
WLON = 12
LAT_DEV = 6
NLAT = 96
NLON = 192
N_LAT = 16


def set_ends(values, stream_key, least, top_value):
    longest = values.shape.index(max(values.shape))
    spots = []
    for shift in (0, 1):
        where = [jax.random.randint(jax.random.fold_in(stream_key, axis), (), 0, length) for axis, length in enumerate(values.shape)]
        where[longest] = (where[longest] + shift) % values.shape[longest]
        spots.append(tuple(where))
    return values.at[spots[0]].set(least).at[spots[1]].set(top_value)


def levels(stream_key, shape, pieces, least, high):
    level, own = 1.0, jax.random.fold_in(stream_key, 6)
    for dim, parts in pieces:
        heights = jnp.exp(jax.random.uniform(jax.random.fold_in(own, dim), (parts,), jnp.float32, least / len(pieces), high / len(pieces)))
        level = level * jnp.repeat(heights, shape[dim] // parts).reshape([-1 if axis == dim else 1 for axis in range(len(shape))])
    return level


def gaussian(rng, dims, scale, limit, split=(), kind=jnp.bfloat16):
    values = jax.random.normal(rng, dims, jnp.float32) * scale
    if len(split) > 0:
        values = levels(rng, dims, split, -0.22, 0.18) * values
    return jnp.clip(values, min=-limit, max=limit).astype(kind)


def setup_inputs(seed: int = 0) -> dict:
    arg_keys = jax.random.split(jax.random.key(seed), 19)
    return {
        "levels_in": gaussian(arg_keys[0], (LEVELS, NLAT, NLON, D), 1.0, 6.0, ((1, 16), (2, 16))),
        "surface": gaussian(arg_keys[1], (NLAT, NLON, D), 1.0, 6.0, ((0, 16), (1, 16))),
        "latents": gaussian(arg_keys[2], (LATENT, D), 0.5, 3.0),
        "level_codes": gaussian(arg_keys[3], (LEVELS, D), 0.5, 3.0),
        "norm_gains": jnp.clip(1.0 + 0.18 * jax.random.normal(arg_keys[4], (6, D), jnp.float32), 0.1, 1.9),
        "agg_query_w": gaussian(arg_keys[5], (D, D), D ** -0.5, 0.25, ((0, 16),)),
        "agg_key_w": gaussian(arg_keys[6], (D, D), D ** -0.5, 0.25, ((0, 16),)),
        "agg_value_w": gaussian(arg_keys[7], (D, D), D ** -0.5, 0.25, ((0, 16),)),
        "agg_out_w": gaussian(arg_keys[8], (D, D), D ** -0.5, 0.25, ((0, 16),)),
        "dec_query_w": gaussian(arg_keys[9], (D, D), D ** -0.5, 0.25, ((0, 16),)),
        "dec_key_w": gaussian(arg_keys[10], (D, D), D ** -0.5, 0.25, ((0, 16),)),
        "dec_value_w": gaussian(arg_keys[11], (D, D), D ** -0.5, 0.25, ((0, 16),)),
        "dec_out_w": gaussian(arg_keys[12], (D, D), D ** -0.5, 0.25, ((0, 16),)),
        "qkv_w": gaussian(arg_keys[13], (2, D, 3 * D), D ** -0.5, 0.25, ((1, 16),)),
        "proj_w": gaussian(arg_keys[14], (2, D, D), D ** -0.5, 0.25, ((1, 16),)),
        "mlp_in": gaussian(arg_keys[15], (2, FF, D), D ** -0.5, 0.25, ((1, 16),)),
        "mlp_out": gaussian(arg_keys[16], (2, FF, D), FF ** -0.5, 0.125, ((1, 16),)),
        "regions": set_ends(jax.random.randint(arg_keys[17], (ZL, NLAT), 0, 3), jax.random.fold_in(arg_keys[17], 1), 0, 2).astype(jnp.int32),
    }


NORM_EPSILON = 1e-05
TOP_PRECISION = lax.Precision.HIGHEST

def layer_norm(values, gain_row):
    widened = values.astype(jnp.float32)
    centre = widened - lax.optimization_barrier(jnp.mean(widened, axis=-1, keepdims=True))
    variance = lax.optimization_barrier(jnp.mean(centre * centre, axis=-1, keepdims=True))
    return (centre * lax.rsqrt(variance + NORM_EPSILON) * gain_row).astype(jnp.bfloat16)

def head_matrix(queries):
    query_count = queries.shape[0]
    identity = (jnp.arange(HEADS)[:, None] == jnp.arange(HEADS)[None, :]).astype(jnp.float32)
    blocked = queries.reshape(query_count, HEADS, HD)[:, :, :, None] * identity[None, :, None, :]
    return jnp.transpose(blocked, (1, 2, 0, 3)).reshape(HEADS * HD, query_count * HEADS)

def attend_levels(key_rows, value_rows, queries, level_count):
    score_scale = HD ** (-0.5)
    scores = jnp.dot(key_rows, head_matrix(queries), precision=TOP_PRECISION, preferred_element_type=jnp.float32) * score_scale
    scores = scores.reshape(level_count, -1, queries.shape[0], HEADS)
    exponent = jnp.exp(scores)
    weights_bf = (exponent / lax.optimization_barrier(jnp.sum(exponent, axis=0, keepdims=True))).astype(jnp.bfloat16)
    spread = jnp.repeat(weights_bf, HD, axis=-1).astype(jnp.float32)
    values_wide = value_rows.reshape(level_count, -1, 1, value_rows.shape[-1]).astype(jnp.float32)
    return lax.optimization_barrier(jnp.sum(spread * values_wide, axis=0)).astype(jnp.bfloat16)

def merge_out(mixed_rows, base_rows, out_weight):
    points, query_count, feature_width = mixed_rows.shape
    stacked = jnp.transpose(mixed_rows, (1, 0, 2)).reshape(query_count * points, feature_width)
    projected = jnp.dot(stacked, out_weight, preferred_element_type=jnp.float32).reshape(query_count, points, feature_width)
    return (base_rows.astype(jnp.float32)[:, None, :] + projected).astype(jnp.bfloat16)

def to_windows(level_grid):
    lev_count, row_count, col_count, last_size = level_grid.shape
    regrouped = level_grid.reshape(lev_count // WZ, WZ, row_count // WLAT, WLAT, col_count // WLON, WLON, last_size)
    return jnp.transpose(regrouped, (0, 2, 4, 1, 3, 5, 6)).reshape(-1, WZ * WLAT * WLON, last_size)

def from_windows(windows, lev_count, row_count, col_count):
    last_size = windows.shape[-1]
    regrouped = windows.reshape(lev_count // WZ, row_count // WLAT, col_count // WLON, WZ, WLAT, WLON, last_size)
    return jnp.transpose(regrouped, (0, 3, 1, 4, 2, 5, 6)).reshape(lev_count, row_count, col_count, last_size)

def window_ids(region_rows, col_count):
    lev_count, row_count = region_rows.shape
    id_grid = jnp.broadcast_to(region_rows[:, :, None, None], (lev_count, row_count, col_count, 1))
    return to_windows(id_grid)[:, :, 0]

def window_attention(packed, window_id):
    feature_width = packed.shape[-1] // 3
    win_count, win_size = (packed.shape[0], packed.shape[1])

    def heads_of(which_part):
        section = packed[:, :, which_part * feature_width:(which_part + 1) * feature_width]
        return section.reshape(win_count, win_size, HEADS, HD).astype(jnp.float32)
    scores = jnp.einsum('wqhd,wkhd->whqk', heads_of(0), heads_of(1), precision=TOP_PRECISION) * HD ** (-0.5)
    exponent = jnp.exp(scores)
    if window_id is not None:
        exponent = exponent * (window_id[:, None, :, None] == window_id[:, None, None, :]).astype(jnp.float32)
    weights_bf = (exponent / lax.optimization_barrier(jnp.sum(exponent, axis=-1, keepdims=True))).astype(jnp.bfloat16)
    mixed_rows = jnp.einsum('whqk,wkhd->wqhd', weights_bf.astype(jnp.float32), heads_of(2), precision=TOP_PRECISION)
    return mixed_rows.reshape(win_count, win_size, HEADS * HD).astype(jnp.bfloat16)

def swin_band(band_block, window_id, block_weights):
    qkv_weight, proj_weight, in_weight, out_weight, first_gain, second_gain = block_weights
    lev_count, row_count, col_count, feature_width = band_block.shape
    normed = layer_norm(band_block, first_gain).reshape(-1, feature_width)
    packed = jnp.dot(normed, qkv_weight, preferred_element_type=jnp.float32).astype(jnp.bfloat16)
    packed = packed.reshape(lev_count, row_count, col_count, 3 * feature_width)
    attended = from_windows(window_attention(to_windows(packed), window_id), lev_count, row_count, col_count)
    attended = attended.reshape(-1, feature_width)
    residual = band_block.reshape(-1, feature_width).astype(jnp.float32)
    after_attention = (residual + jnp.dot(attended, proj_weight, preferred_element_type=jnp.float32)).astype(jnp.bfloat16)
    second = layer_norm(after_attention, second_gain)
    hidden = jax.nn.gelu(jnp.dot(second, in_weight.T, preferred_element_type=jnp.float32), approximate=False).astype(jnp.bfloat16)
    result = (after_attention.astype(jnp.float32) + jnp.dot(hidden, out_weight, preferred_element_type=jnp.float32)).astype(jnp.bfloat16)
    return result.reshape(lev_count, row_count, col_count, feature_width)

def reference(levels_in, surface, latents, level_codes, norm_gains, agg_query_w, agg_key_w, agg_value_w, agg_out_w, dec_query_w, dec_key_w, dec_value_w, dec_out_w, qkv_w, proj_w, mlp_in, mlp_out, regions):
    agg_query = jnp.dot(latents, agg_query_w, preferred_element_type=jnp.float32)
    dec_query = jnp.dot(level_codes, dec_query_w, preferred_element_type=jnp.float32)
    level_bands = jnp.transpose(levels_in.reshape(LEVELS, N_LAT, LAT_DEV, NLON, D), (1, 0, 2, 3, 4))
    surface_bands = surface.reshape(N_LAT, LAT_DEV, NLON, D)

    def aggregate_band(band_pair):
        band_block, surface_band = band_pair
        token_rows = layer_norm(band_block, norm_gains[0]).reshape(-1, D)
        key_rows = jnp.dot(token_rows, agg_key_w, preferred_element_type=jnp.float32)
        value_rows = jnp.dot(token_rows, agg_value_w, preferred_element_type=jnp.float32).astype(jnp.bfloat16)
        mixed_rows = attend_levels(key_rows, value_rows, agg_query, LEVELS)
        latent = merge_out(mixed_rows, latents, agg_out_w).reshape(LATENT, LAT_DEV, NLON, D)
        return jnp.concatenate([surface_band[None], latent], axis=0)
    latent_grid = lax.map(aggregate_band, (level_bands, surface_bands))
    latent_grid = jnp.transpose(latent_grid, (1, 0, 2, 3, 4)).reshape(ZL, NLAT, NLON, D)
    half_rows = WLAT // 2
    half_cols = WLON // 2
    band_count = NLAT // WLAT
    for block_id in range(2):
        if block_id == 1:
            latent_grid = jnp.roll(latent_grid, (-1, -half_rows, -half_cols), axis=(0, 1, 2))
        band_stack = jnp.transpose(latent_grid.reshape(ZL, band_count, WLAT, NLON, D), (1, 0, 2, 3, 4))
        region_bands = jnp.transpose(regions.reshape(ZL, band_count, WLAT), (1, 0, 2))
        block_weights = (qkv_w[block_id], proj_w[block_id], mlp_in[block_id], mlp_out[block_id], norm_gains[2 + 2 * block_id], norm_gains[3 + 2 * block_id])
        if block_id == 1:
            band_stack = lax.map(lambda band_pair: swin_band(band_pair[0], window_ids(band_pair[1], NLON), block_weights), (band_stack, region_bands))
        else:
            band_stack = lax.map(lambda band_block: swin_band(band_block, None, block_weights), band_stack)
        latent_grid = jnp.transpose(band_stack, (1, 0, 2, 3, 4)).reshape(ZL, NLAT, NLON, D)
        if block_id == 1:
            latent_grid = jnp.roll(latent_grid, (1, half_rows, half_cols), axis=(0, 1, 2))
    atmos_grid = latent_grid[1:]
    atmos_bands = jnp.transpose(atmos_grid.reshape(LATENT, N_LAT, LAT_DEV, NLON, D), (1, 0, 2, 3, 4))

    def decode_band(band_block):
        token_rows = layer_norm(band_block, norm_gains[1]).reshape(-1, D)
        key_rows = jnp.dot(token_rows, dec_key_w, preferred_element_type=jnp.float32)
        value_rows = jnp.dot(token_rows, dec_value_w, preferred_element_type=jnp.float32).astype(jnp.bfloat16)
        mixed_rows = attend_levels(key_rows, value_rows, dec_query, LATENT)
        return merge_out(mixed_rows, level_codes, dec_out_w).reshape(LEVELS, LAT_DEV, NLON, D)
    decoded = lax.map(decode_band, atmos_bands)
    return jnp.transpose(decoded, (1, 0, 2, 3, 4)).reshape(LEVELS, NLAT, NLON, D)
```

```python
import functools

import jax
import jax.numpy as jnp
import numpy as np
from jax import lax
from jax.experimental import pallas as pl
from jax.experimental.pallas import tpu as pltpu
from jax.sharding import PartitionSpec as P

LEVELS = 13
LATENT = 3
HEADS = 16
HD = 32
D = 512
PATCHES = 72
TOKENS = 288
WINDOW = 144
ROWS = 960
SCALE = HD ** (-0.5)
EPSILON = 1e-05
F32 = jnp.float32
BF16 = jnp.bfloat16

CHUNKS = (
    ((("agg_query_w", None), ("agg_key_w", None)), 32, 512, 0, "xy"),
    ((("agg_value_w", None), ("agg_out_w", None)), 32, 512, 1, "yx"),
    ((("qkv_w", 0),), 32, 1536, 0, "xy"),
    ((("proj_w", 0),), 32, 512, 1, "yx"),
    ((("mlp_in", 0),), 128, 512, 0, "xy"),
    ((("mlp_out", 0),), 128, 512, 1, "yx"),
    ((("proj_w", 1),), 32, 512, 0, "xy"),
    ((("qkv_w", 1),), 32, 1536, 1, "yx"),
    ((("mlp_in", 1),), 128, 512, 0, "z"),
    ((("mlp_out", 1),), 128, 512, 1, "z"),
    ((("dec_query_w", None), ("dec_key_w", None)), 32, 512, 0, "xy"),
    ((("dec_value_w", None), ("dec_out_w", None)), 32, 512, 1, "yx"),
)
WEIGHTS = ("agg_query_w", "agg_key_w", "agg_value_w", "agg_out_w", "dec_query_w", "dec_key_w",
           "dec_value_w", "dec_out_w", "qkv_w", "proj_w", "mlp_in", "mlp_out")
ALL = slice(None)


def buffer_shape(chunk):
    return (len(chunk[0]), 8, 2, 2, chunk[1] // 2, chunk[2])


class Place:
    def __init__(self):
        lat, lon = lax.axis_index("lat"), lax.axis_index("lon")
        self.lat, self.lon = lat, lon
        self.z, self.h = lax.div(lat, 2), lax.rem(lat, 2)
        self.y, self.l, self.core = lax.div(lon, 4), lax.rem(lax.div(lon, 2), 2), lax.rem(lon, 2)
        self.x = 2 * self.h + self.l

    def device(self, z=None, x=None, y=None, core=None):
        z = self.z if z is None else z
        x = self.x if x is None else x
        y = self.y if y is None else y
        core = self.core if core is None else core
        return {"lat": 2 * z + lax.div(x, 2), "lon": 4 * y + 2 * lax.rem(x, 2) + core}

    def beside(self, lat_step, lon_step):
        return {"lat": lax.rem(self.lat + lat_step + 16, 16), "lon": lax.rem(self.lon + lon_step + 16, 16)}

    def turn(self, axis, step):
        size = 8 if axis == "z" else 4
        return lax.rem(getattr(self, axis) + step + size, size)


def remote(src, dst, send_sem, recv_sem, device):
    return pltpu.make_async_remote_copy(src_ref=src, dst_ref=dst, send_sem=send_sem, recv_sem=recv_sem,
                                        device_id=device, device_id_type=pl.DeviceIdType.MESH)


def wait_bytes(ref, sem):
    pltpu.make_async_copy(ref, ref, sem).wait()


class Carrier:
    def __init__(self, place, chunk, sources, buf, index, send, recv, core_recv):
        self.place, self.chunk, self.sources, self.buf, self.index = place, chunk, sources, buf, index
        self.send, self.recv, self.core_recv = send, recv, core_recv
        self.core, self.kind = chunk[3], chunk[4]
        self.last = 5 if self.kind == "z" else 4
        self.done = 0

    def cols(self, y):
        width = self.chunk[2] // 4
        return pl.ds(pl.multiple_of(y * width, 128), width)

    def part(self, stage, c, zs=ALL):
        d1, d2 = self.kind
        at = {d2: c}
        if stage == 1:
            at = {d1: c, d2: getattr(self.place, d2)}
        x, y = at.get("x"), at.get("y")
        hl = (ALL, ALL) if x is None else (lax.div(x, 2), lax.rem(x, 2))
        return self.buf.at[(ALL, zs) + hl + (ALL, ALL if y is None else self.cols(y))]

    def to(self, ref, slot, **where):
        return remote(ref, ref, self.send.at[self.index, slot], self.recv.at[self.index, slot],
                      self.place.device(**where))

    def to_core(self, ref, k):
        return remote(ref, ref, self.send.at[self.index, 9 + k], self.core_recv.at[self.index, k],
                      self.place.device(core=1 - self.place.core))

    def first_copies(self):
        p, half = self.place, self.chunk[1] // 2
        local, away = [], []
        for k, src in enumerate(self.sources):
            if self.kind == "z":
                for n in range(2):
                    s, d = src.at[pl.ds(n * half, half)], self.buf.at[k, p.z, p.h, n]
                    local.append(pltpu.make_async_copy(s, d, self.send.at[self.index, 17]))
                    away.append(remote(s, d, self.send.at[self.index, 0], self.recv.at[self.index, 0],
                                       p.device(x=lax.rem(p.x + 3 + 2 * p.l, 4))))
            else:
                s = src.at[pl.ds(pl.multiple_of(p.l * half, 16), half), self.cols(p.y)]
                d = self.buf.at[k, p.z, p.h, p.l, :, self.cols(p.y)]
                local.append(pltpu.make_async_copy(s, d, self.send.at[self.index, 17]))
                for step in range(1, 8):
                    away.append(remote(s, d, self.send.at[self.index, 0], self.recv.at[self.index, 0],
                                       p.device(z=p.turn("z", step))))
        return local, away

    def first_size(self):
        p = self.place
        if self.kind == "z":
            return self.buf.at[:, p.z, p.h]
        return self.buf.at[:, pl.ds(0, 7), p.h, p.l, :, self.cols(p.y)]

    def copies(self, task):
        p = self.place
        if self.kind == "z":
            if task == 1:
                own = self.buf.at[:, p.z]
                return [(None, self.to(own, 1, z=p.turn("z", 1))), (None, self.to(own, 2, z=p.turn("z", -1))),
                        (None, self.to_core(own, 0))]
            if task == 5:
                far = p.turn("z", 4)
                return [((self.buf.at[:, far, 0], 7), None), ((self.buf.at[:, far, 1], 8), None),
                        (None, self.to_core(self.buf.at[:, far], 7))]
            found = []
            for n, sign in enumerate((1, -1)):
                c = p.turn("z", sign * (1 - task))
                slab = self.buf.at[:, c]
                onward = self.buf.at[:, c, n] if task == 4 else slab
                found.append(((slab, 2 * task - 3 + n), self.to(onward, 2 * task - 1 + n, z=p.turn("z", sign))))
                found.append((None, self.to_core(slab, 2 * task - 3 + n)))
            return found
        d1, d2 = self.kind
        if task == 1:
            own = self.part(1, getattr(p, d1))
            return [(None, self.to(own, 1, **{d1: p.turn(d1, 1)})), (None, self.to(own, 2, **{d1: p.turn(d1, -1)})),
                    (None, self.to(own, 3, **{d1: p.turn(d1, 2)}))]
        up, down, far = p.turn(d2, 1), p.turn(d2, -1), p.turn(d2, 2)
        low, high = pl.ds(0, 4), pl.ds(4, 4)
        if task == 2:
            own = self.part(2, getattr(p, d2))
            return [((self.part(1, p.turn(d1, -1)), 1), None), ((self.part(1, p.turn(d1, 1)), 2), None),
                    ((self.part(1, p.turn(d1, 2)), 3), None),
                    (None, self.to(own, 5, **{d2: up})), (None, self.to(own, 6, **{d2: down})),
                    (None, self.to_core(own, 0))]
        if task == 3:
            return [((self.part(2, down), 5), self.to(self.part(2, down, low), 7, **{d2: up})),
                    ((self.part(2, up), 6), self.to(self.part(2, up, high), 8, **{d2: down})),
                    (None, self.to_core(self.part(2, down), 1)), (None, self.to_core(self.part(2, up), 2))]
        return [((self.part(2, far, low), 7), None), ((self.part(2, far, high), 8), None),
                (None, self.to_core(self.part(2, far), 3))]

    def run(self, task):
        assert task == self.done, (self.chunk, task)
        self.done += 1

        @pl.when(self.place.core == self.core)
        def _():
            p = self.place
            if task == 0:
                local, away = self.first_copies()
                for copy in away + local:
                    copy.start()
                return
            if task == 1:
                own = self.buf.at[:, p.z, p.h]
                if self.kind != "z":
                    own = self.buf.at[:, p.z, p.h, p.l, :, self.cols(p.y)]
                wait_bytes(own, self.send.at[self.index, 17])
                wait_bytes(self.first_size(), self.recv.at[self.index, 0])
            for before, copy in self.copies(task):
                if before is not None:
                    wait_bytes(before[0], self.recv.at[self.index, before[1]])
                if copy is not None:
                    copy.start()

    def finish(self):
        @pl.when(self.place.core == self.core)
        def _():
            wait_bytes(self.first_size(), self.send.at[self.index, 0])
            for task in range(1, self.last + 1):
                for _, copy in self.copies(task):
                    if copy is not None:
                        copy.wait_send()

    def arrived(self):
        assert self.done == self.last + 1, self.chunk
        p = self.place

        @pl.when(p.core != self.core)
        def _():
            if self.kind == "z":
                refs = [self.buf.at[:, p.turn("z", n)] for n in (0, -1, 1, -2, 2, -3, 3, 4)]
            else:
                d2 = self.kind[1]
                refs = [self.part(2, p.turn(d2, n)) for n in (0, -1, 1, 2)]
            for k, ref in enumerate(refs):
                wait_bytes(ref, self.core_recv.at[self.index, k])


def normed(values, gain):
    centre = values - jnp.mean(values, axis=-1, keepdims=True)
    variance = jnp.mean(centre * centre, axis=-1, keepdims=True)
    return (centre * lax.rsqrt(variance + EPSILON) * gain).astype(BF16)


def dot(a, b):
    return jnp.dot(a, b, preferred_element_type=F32)


def dot_t(a, b):
    return lax.dot_general(a, b, (((1,), (1,)), ((), ())), preferred_element_type=F32)


def gelu(values):
    return (0.5 * values * (1.0 + lax.erf(values * (0.5 ** 0.5)))).astype(BF16)


def rounded(values):
    return values.astype(BF16).astype(F32)


def split(values):
    high = values.astype(BF16)
    return high, (values - high.astype(F32)).astype(BF16)


def lane_head(shape):
    return lax.div(lax.broadcasted_iota(jnp.int32, shape, len(shape) - 1), HD)


def head_rows(queries, count):
    own = lax.broadcasted_iota(jnp.int32, (HEADS, D), 0) == lane_head((HEADS, D))
    return jnp.concatenate([jnp.where(own, queries[n:n + 1], 0.0) for n in range(count)], axis=0)


def spread_matrix(rows, first):
    shape = (rows, D)
    own = lax.broadcasted_iota(jnp.int32, shape, 0) - first == lane_head(shape)
    return jnp.where(own, 1.0, 0.0).astype(BF16)


def score_matrix(queries, count, query_w, key_w, high_ref, low_ref):
    high, low = split(head_rows(dot(queries, query_w), count))
    high_ref[...], low_ref[...] = split(dot_t(key_w, high) + dot_t(key_w, low))


def rows_of(index, size):
    return pl.ds(pl.multiple_of(index * size, size & -size), size)


def norm_rows(src, dst, gain, rows, block=48):
    def step(n, _):
        dst[rows_of(n, block)] = normed(src[rows_of(n, block)], gain)
        return 0
    lax.fori_loop(0, rows // block, step, 0, unroll=True)


def attention(packed, attended, masks):
    lane = lane_head((WINDOW, 128))
    ones = jnp.ones((WINDOW, 128), BF16)

    def step(n, _):
        w, g = lax.div(n, 4), lax.rem(n, 4)
        rows = rows_of(w, WINDOW)
        q, k, v = (packed[rows, pl.ds(pl.multiple_of(g * 128 + part * D, 128), 128)] for part in range(3))
        heads = [jnp.where(lane == m, q, jnp.zeros_like(q)) for m in range(4)]
        weights = []
        for m in range(4):
            e = jnp.exp(dot_t(heads[m], k) * SCALE)
            if masks is not None:
                e = e * masks[w]
            weights.append(e.astype(BF16))
        both = jnp.concatenate([v, ones], axis=1)
        total = jnp.zeros((WINDOW, 128), F32)
        for m in range(4):
            mixed = dot(weights[m], both)
            total = jnp.where(lane == m, mixed[:, :128] / mixed[:, 128:], total)
        attended[rows, pl.ds(pl.multiple_of(g * 128, 128), 128)] = total.astype(BF16)
        return 0
    lax.fori_loop(0, 8, step, 0)


def kernel(plan, *refs):
    (levels_ref, surface_ref, latents_ref, codes_ref, gains_ref, regions_ref), refs = refs[:6], refs[6:]
    sources, refs = dict(zip(WEIGHTS, refs[:12])), refs[12:]
    (pack1, open1, pack2, open2), refs = refs[:4], refs[4:]
    out_ref, refs = refs[0], refs[1:]
    buffers, refs = refs[:len(CHUNKS)], refs[len(CHUNKS):]
    (send, recv, core_recv, halo_send, halo_recv, stage, norm, values, expo, fa_high, fa_low, fd_high, fd_low,
     grid, packed, attended, grid_norm, total, masks, out1, in1, out2, in2, dec_expo) = refs

    place = Place()
    barrier = pltpu.get_barrier_semaphore()
    friends = [place.device(z=place.turn("z", n)) for n in range(1, 8)]
    friends += [place.device(x=place.turn("x", n)) for n in range(1, 4)]
    friends += [place.device(y=place.turn("y", n)) for n in range(1, 4)]
    friends += [place.device(core=1 - place.core)]
    friends += [place.beside(i, j) for i, j in ((1, 0), (0, 1), (1, 1), (-1, 0), (0, -1), (-1, -1))]
    for friend in friends:
        pl.semaphore_signal(barrier, inc=1, device_id=friend, device_id_type=pl.DeviceIdType.MESH)
    pl.semaphore_wait(barrier, len(friends))

    carriers, count = [], [0, 0]
    for chunk, buf in zip(CHUNKS, buffers):
        own = [sources[w] if k is None else sources[w].at[k] for w, k in chunk[0]]
        carriers.append(Carrier(place, chunk, own, buf, count[chunk[3]], send, recv, core_recv))
        count[chunk[3]] += 1
    pairs = list(zip(carriers[0::2], carriers[1::2]))

    def pump(point):
        for pair, task in plan.get(point, ()):
            for carrier in pairs[pair]:
                carrier.run(task)

    def weight(n, k=0):
        buf = buffers[n]
        return buf[k].reshape(16 * CHUNKS[n][1], CHUNKS[n][2])

    def ready(*numbers):
        for n in numbers:
            carriers[n].arrived()

    pump("start")
    stage[936:960] = jnp.zeros((24, D), F32)
    for level in range(LEVELS):
        for i in range(6):
            stage[PATCHES * level + 12 * i:PATCHES * level + 12 * i + 12] = levels_ref[level, i].astype(F32)
    for i in range(6):
        grid[12 * i:12 * i + 12] = surface_ref[i].astype(F32)
    pump("compact")
    norm_rows(stage, norm, gains_ref[0:1], ROWS)
    pump("norm")
    ready(0)
    score_matrix(latents_ref[...], LATENT, weight(0, 0), weight(0, 1), fa_high, fa_low)
    pump("agg_matrix")

    def score_step(n, _):
        block = norm[rows_of(n, 192)]
        expo[rows_of(n, 192)] = jnp.exp((dot(block, fa_high[...]) + dot(block, fa_low[...])) * SCALE)
        return 0
    lax.fori_loop(0, ROWS // 192, score_step, 0)
    pump("agg_scores")
    ready(1)

    def value_step(n, _):
        values[rows_of(n, 192)] = dot(norm[rows_of(n, 192)], weight(1, 0))
        return 0
    lax.fori_loop(0, ROWS // 192, value_step, 0)
    pump("agg_values")
    inverse = 1.0 / lax.fori_loop(
        0, LEVELS, lambda n, s: s + expo[rows_of(n, PATCHES)], jnp.zeros((PATCHES, LATENT * HEADS), F32))
    for a in range(LATENT):
        spread = spread_matrix(LATENT * HEADS, HEADS * a)

        def mix_step(n, s):
            probs = (expo[rows_of(n, PATCHES)] * inverse).astype(BF16)
            return s + dot(probs, spread) * values[rows_of(n, PATCHES)]
        mixed = lax.fori_loop(0, LEVELS, mix_step, jnp.zeros((PATCHES, D), F32))
        total[PATCHES * a:PATCHES * a + PATCHES] = mixed
        pump("agg_mix%d" % a)
    projected = dot(total[0:216].astype(BF16), weight(1, 1))
    for a in range(LATENT):
        rows = projected[PATCHES * a:PATCHES * a + PATCHES]
        grid[PATCHES * (a + 1):PATCHES * (a + 2)] = rounded(latents_ref[a:a + 1].astype(F32) + rows)
    pump("agg_out")

    def block(b):
        name = "b%d_" % b
        norm_rows(grid, grid_norm, gains_ref[2 + 2 * b:3 + 2 * b], TOKENS)
        qkv_n, proj_n = (7, 6) if b else (2, 3)
        in_n, out_n = (8, 9) if b else (4, 5)
        ready(qkv_n)
        for n in range(6):
            cols = buffers[qkv_n][0, :, :, :, :, 256 * n:256 * n + 256].reshape(D, 256)
            packed[:, 256 * n:256 * n + 256] = dot(grid_norm[...], cols).astype(BF16)
        pump(name + "qkv")
        attention(packed, attended, masks if b else None)
        pump(name + "attention")
        ready(proj_n)
        grid[...] = rounded(grid[...] + dot(attended[...], weight(proj_n)))
        pump(name + "proj")
        norm_rows(grid, grid_norm, gains_ref[3 + 2 * b:4 + 2 * b], TOKENS)
        ready(in_n, out_n)
        total[...] = grid[...]

        def step(n, _):
            hidden = gelu(dot_t(grid_norm[...], buffers[in_n][0, n].reshape(256, D)))
            total[...] += dot(hidden, buffers[out_n][0, n].reshape(256, D))
            return 0
        for part in range(4):
            lax.fori_loop(2 * part, 2 * part + 2, step, 0)
            pump(name + "mlp%d" % part)

    block(0)

    def exchange(source, target, size, slot, own, sends):
        keep = pltpu.make_async_copy(source.at[pl.ds(own * size, size)], target.at[pl.ds(own * size, size)],
                                     halo_send.at[slot, 3])
        copies = [remote(source.at[pl.ds(q * size, size)], target.at[pl.ds(q * size, size)], halo_send.at[slot, n],
                         halo_recv.at[slot, n], place.beside(i, j)) for n, (q, i, j) in enumerate(sends)]
        for copy in copies:
            copy.start()
        keep.start()
        return copies, keep

    out1[...] = dot(pack1[...], total[...].astype(BF16)).astype(BF16)
    copies, keep = exchange(out1, in1, 80, 0, 3, ((1, -1, 0), (2, 0, -1), (0, -1, -1)))
    pump("halo1")
    ids = [[regions_ref[level, i] for i in range(6)] for level in range(4)]
    for w in range(2):
        rows_id = jnp.zeros((WINDOW, WINDOW), jnp.int32)
        cols_id = jnp.zeros((WINDOW, WINDOW), jnp.int32)
        for n in range(12):
            value = ids[2 * w + n // 6][n % 6]
            rows_id = jnp.where(lax.broadcasted_iota(jnp.int32, (WINDOW, WINDOW), 0) >= 12 * n, value, rows_id)
            cols_id = jnp.where(lax.broadcasted_iota(jnp.int32, (WINDOW, WINDOW), 1) >= 12 * n, value, cols_id)
        masks[w] = jnp.where(rows_id == cols_id, 1.0, 0.0)
    for copy in copies:
        copy.wait()
    keep.wait()
    grid[...] = dot(open1[...], in1[...])
    block(1)
    out2[...] = dot(pack2[...], total[...].astype(BF16)).astype(BF16)
    copies, keep = exchange(out2, in2, 64, 1, 0, ((2, 1, 0), (1, 0, 1), (3, 1, 1)))
    pump("halo2")
    ready(10)
    score_matrix(codes_ref[...], LEVELS, weight(10, 0), weight(10, 1), fd_high, fd_low)
    for copy in copies:
        copy.wait()
    keep.wait()
    atmos = normed(dot(open2[...], in2[...]), gains_ref[1:2])
    expos = jnp.exp((dot(atmos, fd_high[...]) + dot(atmos, fd_low[...])) * SCALE)
    inverse = 1.0 / (expos[:PATCHES] + expos[PATCHES:2 * PATCHES] + expos[2 * PATCHES:])
    dec_expo[...] = expos * jnp.concatenate([inverse] * LATENT, axis=0)
    ready(11)
    total[0:216] = dot(atmos, weight(11, 0))

    def decode_step(n, _):
        spread = spread_matrix(LEVELS * HEADS, HEADS * n)
        wide = dot(dec_expo[...].astype(BF16), spread) * total[0:216]
        stage[rows_of(n, PATCHES)] = wide[:PATCHES] + wide[PATCHES:2 * PATCHES] + wide[2 * PATCHES:]
        return 0
    lax.fori_loop(0, LEVELS, decode_step, 0)

    def out_step(n, _):
        values[rows_of(n, 192)] = dot(stage[rows_of(n, 192)].astype(BF16), weight(11, 1))
        return 0
    lax.fori_loop(0, ROWS // 192, out_step, 0)
    for level in range(LEVELS):
        code = codes_ref[level:level + 1].astype(F32)
        for i in range(6):
            rows = values[PATCHES * level + 12 * i:PATCHES * level + 12 * i + 12]
            out_ref[level, i] = (code + rows).astype(BF16)
    for carrier in carriers:
        carrier.finish()


def one_hot(targets, sources):
    return (np.asarray(targets)[:, None] == np.arange(sources)[None, :]).astype(np.float32)


def permutations():
    pack_a, open_a, pack_b, open_b = [], [], [], []
    for q in range(4):
        for t in range(80):
            z, i, j = t // 18, t % 18 // 6, t % 6
            pack_a.append(z * 72 + (3 * (q // 2) + i) * 12 + 6 * (q % 2) + j if t < 72 else -1)
        for t in range(64):
            z, i, j = t // 18, t % 18 // 6, t % 6
            pack_b.append(z * 72 + (3 * (q // 2) + i) * 12 + 6 * (q % 2) + j if t < 54 else -1)
    for z in range(4):
        for i in range(6):
            for j in range(12):
                q = 2 * (1 - i // 3) + (1 - j // 6)
                open_a.append(80 * q + (z + 1) % 4 * 18 + i % 3 * 6 + j % 6)
                if z > 0:
                    open_b.append(64 * q + (z - 1) * 18 + i % 3 * 6 + j % 6)
    return one_hot(pack_a, 288), one_hot(open_a, 320), one_hot(pack_b, 288), one_hot(open_b, 256)


PLAN = {
    "start": ((0, 0), (4, 0), (1, 0)),
    "compact": (),
    "norm": ((0, 1), (1, 1), (2, 0), (4, 1), (0, 2), (1, 2), (2, 1), (3, 0), (0, 3), (4, 2), (0, 4)),
    "agg_scores": ((1, 3), (2, 2), (3, 1)),
    "agg_values": ((1, 4), (4, 3), (5, 0)),
    "agg_mix0": ((2, 3), (3, 2)),
    "agg_mix1": ((2, 4),),
    "b0_qkv": ((3, 3), (4, 4), (5, 1)),
    "b0_attention": ((3, 4),),
    "b0_proj": ((4, 5), (5, 2)),
    "b0_mlp1": ((5, 3),),
    "b0_mlp3": ((5, 4),),
}


def body(levels_in, surface, latents, level_codes, norm_gains, agg_query_w, agg_key_w, agg_value_w, agg_out_w,
         dec_query_w, dec_key_w, dec_value_w, dec_out_w, qkv_w, proj_w, mlp_in, mlp_out, regions):
    named = dict(agg_query_w=agg_query_w, agg_key_w=agg_key_w, agg_value_w=agg_value_w, agg_out_w=agg_out_w,
                 dec_query_w=dec_query_w, dec_key_w=dec_key_w, dec_value_w=dec_value_w, dec_out_w=dec_out_w,
                 qkv_w=qkv_w, proj_w=proj_w, mlp_in=mlp_in, mlp_out=mlp_out)
    vmem, smem = pl.BlockSpec(memory_space=pltpu.VMEM), pl.BlockSpec(memory_space=pltpu.SMEM)
    return pl.pallas_call(
        functools.partial(kernel, PLAN),
        out_shape=jax.ShapeDtypeStruct(levels_in.shape, BF16),
        in_specs=[vmem] * 5 + [smem] + [vmem] * 16,
        out_specs=vmem,
        scratch_shapes=[pltpu.VMEM(buffer_shape(chunk), BF16) for chunk in CHUNKS] + [
            pltpu.SemaphoreType.DMA((6, 18)),
            pltpu.SemaphoreType.DMA((6, 9)),
            pltpu.SemaphoreType.DMA((6, 8)),
            pltpu.SemaphoreType.DMA((2, 4)),
            pltpu.SemaphoreType.DMA((2, 3)),
            pltpu.VMEM((ROWS, D), F32),
            pltpu.VMEM((ROWS, D), BF16),
            pltpu.VMEM((ROWS, D), F32),
            pltpu.VMEM((ROWS, LATENT * HEADS), F32),
            pltpu.VMEM((D, LATENT * HEADS), BF16),
            pltpu.VMEM((D, LATENT * HEADS), BF16),
            pltpu.VMEM((D, LEVELS * HEADS), BF16),
            pltpu.VMEM((D, LEVELS * HEADS), BF16),
            pltpu.VMEM((TOKENS, D), F32),
            pltpu.VMEM((TOKENS, 3 * D), BF16),
            pltpu.VMEM((TOKENS, D), BF16),
            pltpu.VMEM((TOKENS, D), BF16),
            pltpu.VMEM((TOKENS, D), F32),
            pltpu.VMEM((2, WINDOW, WINDOW), F32),
            pltpu.VMEM((320, D), BF16),
            pltpu.VMEM((320, D), BF16),
            pltpu.VMEM((256, D), BF16),
            pltpu.VMEM((256, D), BF16),
            pltpu.VMEM((216, LEVELS * HEADS), F32),
        ],
        compiler_params=pltpu.CompilerParams(collective_id=0, has_side_effects=True, vmem_limit_bytes=58 * 2 ** 20),
        cost_estimate=pl.CostEstimate(flops=7 * 10 ** 9, bytes_accessed=10 ** 7, transcendentals=10 ** 7),
    )(levels_in, surface, latents, level_codes, norm_gains, regions, *[named[w] for w in WEIGHTS],
      *[jnp.asarray(m, BF16) for m in permutations()])


def solution(mesh):
    split_rows, split_middle = P("lat", None), P(None, "lat", None)
    in_specs = (P(None, "lat", "lon", None), P("lat", "lon", None), P(), P(), P()) + (split_rows,) * 8 + (
        split_middle,) * 4 + (P(None, "lat"),)
    return jax.shard_map(body, mesh=mesh, in_specs=in_specs, out_specs=P(None, "lat", "lon", None), check_vma=False)
```

```python
import functools

import jax
import jax.numpy as jnp
import numpy as np
from jax import lax
from jax.experimental import pallas as pl
from jax.experimental.pallas import tpu as pltpu
from jax.sharding import PartitionSpec as P

LEVELS = 13
LATENT = 3
HEADS = 16
HD = 32
D = 512
PATCHES = 72
TOKENS = 288
WINDOW = 144
ROWS = 960
SCALE = HD ** (-0.5)
EPSILON = 1e-05
F32 = jnp.float32
BF16 = jnp.bfloat16

CHUNKS = (
    ((("agg_query_w", None), ("agg_key_w", None)), 32, 512, 0, "xy"),
    ((("agg_value_w", None), ("agg_out_w", None)), 32, 512, 1, "yx"),
    ((("qkv_w", 0),), 32, 1536, 0, "xy"),
    ((("proj_w", 0),), 32, 512, 1, "yx"),
    ((("mlp_in", 0),), 128, 512, 0, "xy"),
    ((("mlp_out", 0),), 128, 512, 1, "yx"),
    ((("proj_w", 1),), 32, 512, 0, "xy"),
    ((("qkv_w", 1),), 32, 1536, 1, "yx"),
    ((("mlp_in", 1),), 128, 512, 0, "z"),
    ((("mlp_out", 1),), 128, 512, 1, "z"),
    ((("dec_query_w", None), ("dec_key_w", None)), 32, 512, 0, "xy"),
    ((("dec_value_w", None), ("dec_out_w", None)), 32, 512, 1, "yx"),
)
WEIGHTS = ("agg_query_w", "agg_key_w", "agg_value_w", "agg_out_w", "dec_query_w", "dec_key_w",
           "dec_value_w", "dec_out_w", "qkv_w", "proj_w", "mlp_in", "mlp_out")
ALL = slice(None)


def buffer_shape(chunk):
    return (len(chunk[0]), 8, 2, 2, chunk[1] // 2, chunk[2])


class Place:
    def __init__(self):
        lat, lon = lax.axis_index("lat"), lax.axis_index("lon")
        self.lat, self.lon = lat, lon
        self.z, self.h = lax.div(lat, 2), lax.rem(lat, 2)
        self.y, self.l, self.core = lax.div(lon, 4), lax.rem(lax.div(lon, 2), 2), lax.rem(lon, 2)
        self.x = 2 * self.h + self.l

    def device(self, z=None, x=None, y=None, core=None):
        z = self.z if z is None else z
        x = self.x if x is None else x
        y = self.y if y is None else y
        core = self.core if core is None else core
        return {"lat": 2 * z + lax.div(x, 2), "lon": 4 * y + 2 * lax.rem(x, 2) + core}

    def beside(self, lat_step, lon_step):
        return {"lat": lax.rem(self.lat + lat_step + 16, 16), "lon": lax.rem(self.lon + lon_step + 16, 16)}

    def turn(self, axis, step):
        size = 8 if axis == "z" else 4
        return lax.rem(getattr(self, axis) + step + size, size)


def remote(src, dst, send_sem, recv_sem, device):
    return pltpu.make_async_remote_copy(src_ref=src, dst_ref=dst, send_sem=send_sem, recv_sem=recv_sem,
                                        device_id=device, device_id_type=pl.DeviceIdType.MESH)


def wait_bytes(ref, sem):
    pltpu.make_async_copy(ref, ref, sem).wait()


class Carrier:
    def __init__(self, place, chunk, sources, buf, index, send, recv, core_recv):
        self.place, self.chunk, self.sources, self.buf, self.index = place, chunk, sources, buf, index
        self.send, self.recv, self.core_recv = send, recv, core_recv
        self.core, self.kind = chunk[3], chunk[4]
        self.last = 5 if self.kind == "z" else 4
        self.done = 0

    def cols(self, y):
        width = self.chunk[2] // 4
        return pl.ds(pl.multiple_of(y * width, 128), width)

    def part(self, stage, c, zs=ALL):
        d1, d2 = self.kind
        at = {d2: c}
        if stage == 1:
            at = {d1: c, d2: getattr(self.place, d2)}
        x, y = at.get("x"), at.get("y")
        hl = (ALL, ALL) if x is None else (lax.div(x, 2), lax.rem(x, 2))
        return self.buf.at[(ALL, zs) + hl + (ALL, ALL if y is None else self.cols(y))]

    def to(self, ref, slot, **where):
        return remote(ref, ref, self.send.at[self.index, slot], self.recv.at[self.index, slot],
                      self.place.device(**where))

    def to_core(self, ref, k):
        return remote(ref, ref, self.send.at[self.index, 9 + k], self.core_recv.at[self.index, k],
                      self.place.device(core=1 - self.place.core))

    def first_copies(self):
        p, half = self.place, self.chunk[1] // 2
        local, away = [], []
        for k, src in enumerate(self.sources):
            if self.kind == "z":
                for n in range(2):
                    s, d = src.at[pl.ds(n * half, half)], self.buf.at[k, p.z, p.h, n]
                    local.append(pltpu.make_async_copy(s, d, self.send.at[self.index, 17]))
                    away.append(remote(s, d, self.send.at[self.index, 0], self.recv.at[self.index, 0],
                                       p.device(x=lax.rem(p.x + 3 + 2 * p.l, 4))))
            else:
                s = src.at[pl.ds(pl.multiple_of(p.l * half, 16), half), self.cols(p.y)]
                d = self.buf.at[k, p.z, p.h, p.l, :, self.cols(p.y)]
                local.append(pltpu.make_async_copy(s, d, self.send.at[self.index, 17]))
                for step in range(1, 8):
                    away.append(remote(s, d, self.send.at[self.index, 0], self.recv.at[self.index, 0],
                                       p.device(z=p.turn("z", step))))
        return local, away

    def first_size(self):
        p = self.place
        if self.kind == "z":
            return self.buf.at[:, p.z, p.h]
        return self.buf.at[:, pl.ds(0, 7), p.h, p.l, :, self.cols(p.y)]

    def copies(self, task):
        p = self.place
        if self.kind == "z":
            if task == 1:
                own = self.buf.at[:, p.z]
                return [(None, self.to(own, 1, z=p.turn("z", 1))), (None, self.to(own, 2, z=p.turn("z", -1))),
                        (None, self.to_core(own, 0))]
            if task == 5:
                far = p.turn("z", 4)
                return [((self.buf.at[:, far, 0], 7), None), ((self.buf.at[:, far, 1], 8), None),
                        (None, self.to_core(self.buf.at[:, far], 7))]
            found = []
            for n, sign in enumerate((1, -1)):
                c = p.turn("z", sign * (1 - task))
                slab = self.buf.at[:, c]
                onward = self.buf.at[:, c, n] if task == 4 else slab
                found.append(((slab, 2 * task - 3 + n), self.to(onward, 2 * task - 1 + n, z=p.turn("z", sign))))
                found.append((None, self.to_core(slab, 2 * task - 3 + n)))
            return found
        d1, d2 = self.kind
        if task == 1:
            own = self.part(1, getattr(p, d1))
            return [(None, self.to(own, 1, **{d1: p.turn(d1, 1)})), (None, self.to(own, 2, **{d1: p.turn(d1, -1)})),
                    (None, self.to(own, 3, **{d1: p.turn(d1, 2)}))]
        up, down, far = p.turn(d2, 1), p.turn(d2, -1), p.turn(d2, 2)
        low, high = pl.ds(0, 4), pl.ds(4, 4)
        if task == 2:
            own = self.part(2, getattr(p, d2))
            return [((self.part(1, p.turn(d1, -1)), 1), None), ((self.part(1, p.turn(d1, 1)), 2), None),
                    ((self.part(1, p.turn(d1, 2)), 3), None),
                    (None, self.to(own, 5, **{d2: up})), (None, self.to(own, 6, **{d2: down})),
                    (None, self.to_core(own, 0))]
        if task == 3:
            return [((self.part(2, down), 5), self.to(self.part(2, down, low), 7, **{d2: up})),
                    ((self.part(2, up), 6), self.to(self.part(2, up, high), 8, **{d2: down})),
                    (None, self.to_core(self.part(2, down), 1)), (None, self.to_core(self.part(2, up), 2))]
        return [((self.part(2, far, low), 7), None), ((self.part(2, far, high), 8), None),
                (None, self.to_core(self.part(2, far), 3))]

    def run(self, task):
        assert task == self.done, (self.chunk, task)
        self.done += 1

        @pl.when(self.place.core == self.core)
        def _():
            p = self.place
            if task == 0:
                local, away = self.first_copies()
                for copy in away + local:
                    copy.start()
                return
            if task == 1:
                own = self.buf.at[:, p.z, p.h]
                if self.kind != "z":
                    own = self.buf.at[:, p.z, p.h, p.l, :, self.cols(p.y)]
                wait_bytes(own, self.send.at[self.index, 17])
                wait_bytes(self.first_size(), self.recv.at[self.index, 0])
            for before, copy in self.copies(task):
                if before is not None:
                    wait_bytes(before[0], self.recv.at[self.index, before[1]])
                if copy is not None:
                    copy.start()

    def finish(self):
        @pl.when(self.place.core == self.core)
        def _():
            wait_bytes(self.first_size(), self.send.at[self.index, 0])
            for task in range(1, self.last + 1):
                for _, copy in self.copies(task):
                    if copy is not None:
                        copy.wait_send()

    def arrived(self):
        assert self.done == self.last + 1, self.chunk
        p = self.place

        @pl.when(p.core != self.core)
        def _():
            if self.kind == "z":
                refs = [self.buf.at[:, p.turn("z", n)] for n in (0, -1, 1, -2, 2, -3, 3, 4)]
            else:
                d2 = self.kind[1]
                refs = [self.part(2, p.turn(d2, n)) for n in (0, -1, 1, 2)]
            for k, ref in enumerate(refs):
                wait_bytes(ref, self.core_recv.at[self.index, k])


def normed(values, gain):
    centre = values - jnp.mean(values, axis=-1, keepdims=True)
    variance = jnp.mean(centre * centre, axis=-1, keepdims=True)
    return (centre * lax.rsqrt(variance + EPSILON) * gain).astype(BF16)


def dot(a, b):
    return jnp.dot(a, b, preferred_element_type=F32)


def dot_t(a, b):
    return lax.dot_general(a, b, (((1,), (1,)), ((), ())), preferred_element_type=F32)


def gelu(values):
    return (0.5 * values * (1.0 + lax.erf(values * (0.5 ** 0.5)))).astype(BF16)


def rounded(values):
    return values.astype(BF16).astype(F32)


def split(values):
    high = values.astype(BF16)
    return high, (values - high.astype(F32)).astype(BF16)


def lane_head(shape):
    return lax.div(lax.broadcasted_iota(jnp.int32, shape, len(shape) - 1), HD)


def head_rows(queries, count):
    own = lax.broadcasted_iota(jnp.int32, (HEADS, D), 0) == lane_head((HEADS, D))
    return jnp.concatenate([jnp.where(own, queries[n:n + 1], 0.0) for n in range(count)], axis=0)


def spread_matrix(rows, first):
    shape = (rows, D)
    own = lax.broadcasted_iota(jnp.int32, shape, 0) - first == lane_head(shape)
    return jnp.where(own, 1.0, 0.0).astype(BF16)


def score_matrix(queries, count, query_w, key_w, high_ref, low_ref):
    high, low = split(head_rows(dot(queries, query_w), count))
    high_ref[...], low_ref[...] = split(dot_t(key_w, high) + dot_t(key_w, low))


def rows_of(index, size):
    return pl.ds(pl.multiple_of(index * size, size & -size), size)


def norm_rows(load, dst, gain, rows, block=48):
    def step(n, _):
        dst[rows_of(n, block)] = normed(load(rows_of(n, block)), gain)
        return 0
    lax.fori_loop(0, rows // block, step, 0, unroll=True)


def attention(packed, attended, mask, w):
    lane = lane_head((WINDOW, 128))
    ones = jnp.ones((WINDOW, 128), BF16)
    rows = slice(WINDOW * w, WINDOW * w + WINDOW)
    for g in range(4):
        q, k, v = (packed[rows, 128 * g + part * D:128 * g + part * D + 128] for part in range(3))
        both = jnp.concatenate([v, ones], axis=1)
        total = jnp.zeros((WINDOW, 128), F32)
        for m in range(4):
            e = jnp.exp(dot_t(jnp.where(lane == m, q, jnp.zeros_like(q)), k) * SCALE)
            if mask is not None:
                e = e * mask
            mixed = dot(e.astype(BF16), both)
            total = jnp.where(lane == m, mixed[:, :128] / mixed[:, 128:], total)
        attended[rows, 128 * g:128 * g + 128] = total.astype(BF16)


def kernel(plan, *refs):
    (levels_ref, surface_ref, latents_ref, codes_ref, gains_ref, regions_ref), refs = refs[:6], refs[6:]
    sources, refs = dict(zip(WEIGHTS, refs[:12])), refs[12:]
    (pack1, open1, pack2, open2), refs = refs[:4], refs[4:]
    out_ref, refs = refs[0], refs[1:]
    buffers, refs = refs[:len(CHUNKS)], refs[len(CHUNKS):]
    (send, recv, core_recv, halo_send, halo_recv, tiled, norm, values, expo, fa_high, fa_low, fd_high, fd_low,
     grid, packed, attended, grid_norm, total, masks, out1, in1, out2, in2, dec_expo) = refs

    place = Place()
    barrier = pltpu.get_barrier_semaphore()
    friends = [place.device(z=place.turn("z", n)) for n in range(1, 8)]
    friends += [place.device(x=place.turn("x", n)) for n in range(1, 4)]
    friends += [place.device(y=place.turn("y", n)) for n in range(1, 4)]
    friends += [place.device(core=1 - place.core)]
    friends += [place.beside(i, j) for i, j in ((1, 0), (0, 1), (1, 1), (-1, 0), (0, -1), (-1, -1))]
    for friend in friends:
        pl.semaphore_signal(barrier, inc=1, device_id=friend, device_id_type=pl.DeviceIdType.MESH)

    carriers, count = [], [0, 0]
    for chunk, buf in zip(CHUNKS, buffers):
        own = [sources[w] if k is None else sources[w].at[k] for w, k in chunk[0]]
        carriers.append(Carrier(place, chunk, own, buf, count[chunk[3]], send, recv, core_recv))
        count[chunk[3]] += 1
    pairs = list(zip(carriers[0::2], carriers[1::2]))

    def pump(point):
        for pair, task in plan.get(point, ()):
            for carrier in pairs[pair]:
                carrier.run(task)

    def weight(n, k=0):
        buf = buffers[n]
        return buf[k].reshape(16 * CHUNKS[n][1], CHUNKS[n][2])

    def ready(*numbers):
        for n in numbers:
            carriers[n].arrived()

    tiled[:, 936:960] = jnp.zeros((4, 24, 128), F32)
    for n in range(PATCHES):
        rows = levels_ref[n // 12, n % 12].astype(F32)
        for c in range(4):
            tiled[c, pl.ds(n, LEVELS, stride=PATCHES)] = rows[:, 128 * c:128 * c + 128]
    for i in range(6):
        grid[12 * i:12 * i + 12] = surface_ref[i].astype(F32)
    norm_rows(lambda rows: jnp.concatenate([tiled[c, rows] for c in range(4)], axis=1), norm, gains_ref[0:1], ROWS)
    pl.semaphore_wait(barrier, len(friends))
    pump("start")
    pump("norm")
    ready(0)
    score_matrix(latents_ref[...], LATENT, weight(0, 0), weight(0, 1), fa_high, fa_low)
    pump("agg_matrix")

    def score_step(n, _):
        block = norm[rows_of(n, 192)]
        expo[rows_of(n, 192)] = jnp.exp((dot(block, fa_high[...]) + dot(block, fa_low[...])) * SCALE)
        return 0
    lax.fori_loop(0, ROWS // 192, score_step, 0)
    pump("agg_scores")
    ready(1)

    def value_step(n, _):
        values[rows_of(n, 192)] = dot(norm[rows_of(n, 192)], weight(1, 0))
        return 0
    lax.fori_loop(0, ROWS // 192, value_step, 0)
    pump("agg_values")
    level_rows = [slice(PATCHES * n, PATCHES * n + PATCHES) for n in range(LEVELS)]
    inverse = 1.0 / sum(expo[rows] for rows in level_rows)
    probs = jnp.concatenate([expo[rows] * inverse for rows in level_rows], axis=0).astype(BF16)
    for a in range(LATENT):
        spread = spread_matrix(LATENT * HEADS, HEADS * a)
        for cols in (slice(0, 256), slice(256, 512)):
            wide = dot(probs, spread[:, cols])
            total[PATCHES * a:PATCHES * a + PATCHES, cols] = sum(wide[rows] * values[rows, cols] for rows in level_rows)
        pump("agg_mix%d" % a)
    projected = dot(total[0:216].astype(BF16), weight(1, 1))
    for a in range(LATENT):
        rows = projected[PATCHES * a:PATCHES * a + PATCHES]
        grid[PATCHES * (a + 1):PATCHES * (a + 2)] = rounded(latents_ref[a:a + 1].astype(F32) + rows)
    pump("agg_out")

    def block(b):
        name = "b%d_" % b
        norm_rows(lambda rows: grid[rows], grid_norm, gains_ref[2 + 2 * b:3 + 2 * b], TOKENS)
        qkv_n, proj_n = (7, 6) if b else (2, 3)
        in_n, out_n = (8, 9) if b else (4, 5)
        ready(qkv_n)
        for n in range(6):
            cols = buffers[qkv_n][0, :, :, :, :, 256 * n:256 * n + 256].reshape(D, 256)
            packed[:, 256 * n:256 * n + 256] = dot(grid_norm[...], cols).astype(BF16)
        pump(name + "qkv")
        for w in range(2):
            attention(packed, attended, masks[w] if b else None, w)
            pump(name + "attention%d" % w)
        ready(proj_n)
        grid[...] = rounded(grid[...] + dot(attended[...], weight(proj_n)))
        pump(name + "proj")
        norm_rows(lambda rows: grid[rows], grid_norm, gains_ref[3 + 2 * b:4 + 2 * b], TOKENS)
        ready(in_n, out_n)
        total[...] = grid[...]

        for part in range(4):
            hidden = [gelu(dot_t(grid_norm[...], buffers[in_n][0, n].reshape(256, D)))
                      for n in (2 * part, 2 * part + 1)]
            total[...] += sum(dot(hidden[n], buffers[out_n][0, 2 * part + n].reshape(256, D)) for n in range(2))
            pump(name + "mlp%d" % part)

    block(0)

    def exchange(source, target, size, slot, own, sends):
        keep = pltpu.make_async_copy(source.at[pl.ds(own * size, size)], target.at[pl.ds(own * size, size)],
                                     halo_send.at[slot, 3])
        copies = [remote(source.at[pl.ds(q * size, size)], target.at[pl.ds(q * size, size)], halo_send.at[slot, n],
                         halo_recv.at[slot, n], place.beside(i, j)) for n, (q, i, j) in enumerate(sends)]
        for copy in copies:
            copy.start()
        keep.start()
        return copies, keep

    out1[...] = dot(pack1[...], total[...].astype(BF16)).astype(BF16)
    copies, keep = exchange(out1, in1, 80, 0, 3, ((1, -1, 0), (2, 0, -1), (0, -1, -1)))
    pump("halo1")
    ids = [[regions_ref[level, i] for i in range(6)] for level in range(4)]
    for w in range(2):
        rows_id = jnp.zeros((WINDOW, WINDOW), jnp.int32)
        cols_id = jnp.zeros((WINDOW, WINDOW), jnp.int32)
        for n in range(12):
            value = ids[2 * w + n // 6][n % 6]
            rows_id = jnp.where(lax.broadcasted_iota(jnp.int32, (WINDOW, WINDOW), 0) >= 12 * n, value, rows_id)
            cols_id = jnp.where(lax.broadcasted_iota(jnp.int32, (WINDOW, WINDOW), 1) >= 12 * n, value, cols_id)
        masks[w] = jnp.where(rows_id == cols_id, 1.0, 0.0)
    for copy in copies:
        copy.wait()
    keep.wait()
    grid[...] = dot(open1[...], in1[...])
    block(1)
    out2[...] = dot(pack2[...], total[...].astype(BF16)).astype(BF16)
    copies, keep = exchange(out2, in2, 64, 1, 0, ((2, 1, 0), (1, 0, 1), (3, 1, 1)))
    pump("halo2")
    ready(10)
    score_matrix(codes_ref[...], LEVELS, weight(10, 0), weight(10, 1), fd_high, fd_low)
    for copy in copies:
        copy.wait()
    keep.wait()
    atmos = normed(dot(open2[...], in2[...]), gains_ref[1:2])
    expos = jnp.exp((dot(atmos, fd_high[...]) + dot(atmos, fd_low[...])) * SCALE)
    inverse = 1.0 / (expos[:PATCHES] + expos[PATCHES:2 * PATCHES] + expos[2 * PATCHES:])
    dec_expo[...] = expos * jnp.concatenate([inverse] * LATENT, axis=0)
    ready(11)
    total[0:216] = dot(atmos, weight(11, 0))

    spread = spread_matrix(HEADS, 0)
    for n in range(LEVELS):
        wide = dot(dec_expo[:, HEADS * n:HEADS * n + HEADS].astype(BF16), spread) * total[0:216]
        values[PATCHES * n:PATCHES * n + PATCHES] = (
            wide[:PATCHES] + wide[PATCHES:2 * PATCHES] + wide[2 * PATCHES:])

    def out_step(n, _):
        rows = dot(values[rows_of(n, 192)].astype(BF16), weight(11, 1))
        for c in range(4):
            tiled[c, rows_of(n, 192)] = rows[:, 128 * c:128 * c + 128]
        return 0
    lax.fori_loop(0, ROWS // 192, out_step, 0)
    codes = codes_ref[...].astype(F32)
    for n in range(PATCHES):
        rows = jnp.concatenate([tiled[c, pl.ds(n, LEVELS, stride=PATCHES)] for c in range(4)], axis=1)
        out_ref[n // 12, n % 12] = (codes + rows).astype(BF16)
    for carrier in carriers:
        carrier.finish()


def one_hot(targets, sources):
    return (np.asarray(targets)[:, None] == np.arange(sources)[None, :]).astype(np.float32)


def permutations():
    pack_a, open_a, pack_b, open_b = [], [], [], []
    for q in range(4):
        for t in range(80):
            z, i, j = t // 18, t % 18 // 6, t % 6
            pack_a.append(z * 72 + (3 * (q // 2) + i) * 12 + 6 * (q % 2) + j if t < 72 else -1)
        for t in range(64):
            z, i, j = t // 18, t % 18 // 6, t % 6
            pack_b.append(z * 72 + (3 * (q // 2) + i) * 12 + 6 * (q % 2) + j if t < 54 else -1)
    for z in range(4):
        for i in range(6):
            for j in range(12):
                q = 2 * (1 - i // 3) + (1 - j // 6)
                open_a.append(80 * q + (z + 1) % 4 * 18 + i % 3 * 6 + j % 6)
                if z > 0:
                    open_b.append(64 * q + (z - 1) * 18 + i % 3 * 6 + j % 6)
    return one_hot(pack_a, 288), one_hot(open_a, 320), one_hot(pack_b, 288), one_hot(open_b, 256)


PLAN = {
    "start": ((0, 0), (4, 0)),
    "norm": ((1, 0), (4, 1), (0, 1), (1, 1), (0, 2), (2, 0), (1, 2), (5, 0), (0, 3), (2, 1), (4, 2),
             (1, 3), (0, 4), (3, 0), (4, 3), (2, 2)),
    "agg_mix0": ((3, 1),),
    "agg_mix2": ((1, 4), (2, 3), (4, 4), (3, 2)),
    "b0_qkv": ((4, 5),),
    "b0_attention0": ((2, 4), (5, 1)),
    "b0_proj": ((3, 3),),
    "b0_mlp1": ((5, 2),),
    "b0_mlp3": ((3, 4),),
    "b1_qkv": ((5, 3),),
    "b1_mlp3": ((5, 4),),
}


def body(levels_in, surface, latents, level_codes, norm_gains, agg_query_w, agg_key_w, agg_value_w, agg_out_w,
         dec_query_w, dec_key_w, dec_value_w, dec_out_w, qkv_w, proj_w, mlp_in, mlp_out, regions):
    named = dict(agg_query_w=agg_query_w, agg_key_w=agg_key_w, agg_value_w=agg_value_w, agg_out_w=agg_out_w,
                 dec_query_w=dec_query_w, dec_key_w=dec_key_w, dec_value_w=dec_value_w, dec_out_w=dec_out_w,
                 qkv_w=qkv_w, proj_w=proj_w, mlp_in=mlp_in, mlp_out=mlp_out)
    vmem, smem = pl.BlockSpec(memory_space=pltpu.VMEM), pl.BlockSpec(memory_space=pltpu.SMEM)
    decoded = pl.pallas_call(
        functools.partial(kernel, PLAN),
        out_shape=jax.ShapeDtypeStruct((6, 12, LEVELS, D), BF16),
        in_specs=[vmem] * 5 + [smem] + [vmem] * 16,
        out_specs=vmem,
        scratch_shapes=[pltpu.VMEM(buffer_shape(chunk), BF16) for chunk in CHUNKS] + [
            pltpu.SemaphoreType.DMA((6, 18)),
            pltpu.SemaphoreType.DMA((6, 9)),
            pltpu.SemaphoreType.DMA((6, 8)),
            pltpu.SemaphoreType.DMA((2, 4)),
            pltpu.SemaphoreType.DMA((2, 3)),
            pltpu.VMEM((4, ROWS, 128), F32),
            pltpu.VMEM((ROWS, D), BF16),
            pltpu.VMEM((ROWS, D), F32),
            pltpu.VMEM((ROWS, LATENT * HEADS), F32),
            pltpu.VMEM((D, LATENT * HEADS), BF16),
            pltpu.VMEM((D, LATENT * HEADS), BF16),
            pltpu.VMEM((D, LEVELS * HEADS), BF16),
            pltpu.VMEM((D, LEVELS * HEADS), BF16),
            pltpu.VMEM((TOKENS, D), F32),
            pltpu.VMEM((TOKENS, 3 * D), BF16),
            pltpu.VMEM((TOKENS, D), BF16),
            pltpu.VMEM((TOKENS, D), BF16),
            pltpu.VMEM((TOKENS, D), F32),
            pltpu.VMEM((2, WINDOW, WINDOW), F32),
            pltpu.VMEM((320, D), BF16),
            pltpu.VMEM((320, D), BF16),
            pltpu.VMEM((256, D), BF16),
            pltpu.VMEM((256, D), BF16),
            pltpu.VMEM((216, LEVELS * HEADS), F32),
        ],
        compiler_params=pltpu.CompilerParams(collective_id=0, has_side_effects=True, vmem_limit_bytes=58 * 2 ** 20),
        cost_estimate=pl.CostEstimate(flops=7 * 10 ** 9, bytes_accessed=10 ** 7, transcendentals=10 ** 7),
    )(jnp.transpose(levels_in, (1, 2, 0, 3)), surface, latents, level_codes, norm_gains, regions, *[named[w] for w in WEIGHTS],
      *[jnp.asarray(m, BF16) for m in permutations()])
    return jnp.transpose(decoded, (2, 0, 1, 3))


def solution(mesh):
    split_rows, split_middle = P("lat", None), P(None, "lat", None)
    in_specs = (P(None, "lat", "lon", None), P("lat", "lon", None), P(), P(), P()) + (split_rows,) * 8 + (
        split_middle,) * 4 + (P(None, "lat"),)
    return jax.shard_map(body, mesh=mesh, in_specs=in_specs, out_specs=P(None, "lat", "lon", None), check_vma=False)
```

```python
import functools

import jax
import jax.numpy as jnp
import numpy as np
from jax import lax
from jax.experimental import pallas as pl
from jax.experimental.pallas import tpu as pltpu
from jax.sharding import PartitionSpec as P

LEVELS = 13
LATENT = 3
HEADS = 16
HD = 32
D = 512
PATCHES = 72
TOKENS = 288
WINDOW = 144
ROWS = 960
SCALE = HD ** (-0.5)
EPSILON = 1e-05
F32 = jnp.float32
BF16 = jnp.bfloat16

CHUNKS = (
    ((("agg_query_w", None), ("agg_key_w", None)), 32, 512, 0, "xyu"),
    ((("agg_value_w", None), ("agg_out_w", None)), 32, 512, 1, "yxu"),
    ((("qkv_w", 0),), 32, 1536, 0, "xy"),
    ((("proj_w", 0),), 32, 512, 1, "yx"),
    ((("mlp_in", 0),), 128, 512, 0, "z"),
    ((("mlp_out", 0),), 128, 512, 1, "z"),
    ((("proj_w", 1),), 32, 512, 0, "xy"),
    ((("qkv_w", 1),), 32, 1536, 1, "yx"),
    ((("mlp_in", 1),), 128, 512, 0, "xy"),
    ((("mlp_out", 1),), 128, 512, 1, "yx"),
    ((("dec_query_w", None), ("dec_key_w", None)), 32, 512, 0, "xy"),
    ((("dec_value_w", None), ("dec_out_w", None)), 32, 512, 1, "yx"),
)
WEIGHTS = ("agg_query_w", "agg_key_w", "agg_value_w", "agg_out_w", "dec_query_w", "dec_key_w",
           "dec_value_w", "dec_out_w", "qkv_w", "proj_w", "mlp_in", "mlp_out")
ALL = slice(None)


def buffer_shape(chunk):
    return (len(chunk[0]), 8, 2, 2, chunk[1] // 2, chunk[2])


class Place:
    def __init__(self):
        lat, lon = lax.axis_index("lat"), lax.axis_index("lon")
        self.lat, self.lon = lat, lon
        self.z, self.h = lax.div(lat, 2), lax.rem(lat, 2)
        self.y, self.l, self.core = lax.div(lon, 4), lax.rem(lax.div(lon, 2), 2), lax.rem(lon, 2)
        self.x = 2 * self.h + self.l

    def device(self, z=None, x=None, y=None, core=None):
        z = self.z if z is None else z
        x = self.x if x is None else x
        y = self.y if y is None else y
        core = self.core if core is None else core
        return {"lat": 2 * z + lax.div(x, 2), "lon": 4 * y + 2 * lax.rem(x, 2) + core}

    def beside(self, lat_step, lon_step):
        return {"lat": lax.rem(self.lat + lat_step + 16, 16), "lon": lax.rem(self.lon + lon_step + 16, 16)}

    def turn(self, axis, step):
        size = 8 if axis == "z" else 4
        return lax.rem(getattr(self, axis) + step + size, size)


def remote(src, dst, send_sem, recv_sem, device):
    return pltpu.make_async_remote_copy(src_ref=src, dst_ref=dst, send_sem=send_sem, recv_sem=recv_sem,
                                        device_id=device, device_id_type=pl.DeviceIdType.MESH)


def wait_bytes(ref, sem):
    pltpu.make_async_copy(ref, ref, sem).wait()


class Carrier:
    def __init__(self, place, chunk, sources, buf, index, send, recv, core_recv):
        self.place, self.chunk, self.sources, self.buf, self.index = place, chunk, sources, buf, index
        self.send, self.recv, self.core_recv = send, recv, core_recv
        self.core, self.kind = chunk[3], chunk[4]
        self.last = 5 if self.kind == "z" else 3 if self.kind.endswith("u") else 4
        self.done = 0

    def cols(self, y):
        width = self.chunk[2] // 4
        return pl.ds(pl.multiple_of(y * width, 128), width)

    def part(self, stage, c, zs=ALL):
        d1, d2 = self.kind[:2]
        at = {d2: c}
        if stage == 1:
            at = {d1: c, d2: getattr(self.place, d2)}
        x, y = at.get("x"), at.get("y")
        hl = (ALL, ALL) if x is None else (lax.div(x, 2), lax.rem(x, 2))
        return self.buf.at[(ALL, zs) + hl + (ALL, ALL if y is None else self.cols(y))]

    def to(self, ref, slot, **where):
        return remote(ref, ref, self.send.at[self.index, slot], self.recv.at[self.index, slot],
                      self.place.device(**where))

    def to_core(self, ref, k):
        return remote(ref, ref, self.send.at[self.index, 9 + k], self.core_recv.at[self.index, k],
                      self.place.device(core=1 - self.place.core))

    def first_copies(self):
        p, half = self.place, self.chunk[1] // 2
        local, away = [], []
        for k, src in enumerate(self.sources):
            if self.kind == "z":
                for n in range(2):
                    s, d = src.at[pl.ds(n * half, half)], self.buf.at[k, p.z, p.h, n]
                    local.append(pltpu.make_async_copy(s, d, self.send.at[self.index, 17]))
                    away.append(remote(s, d, self.send.at[self.index, 0], self.recv.at[self.index, 0],
                                       p.device(x=lax.rem(p.x + 3 + 2 * p.l, 4))))
            else:
                s = src.at[pl.ds(pl.multiple_of(p.l * half, 16), half), self.cols(p.y)]
                d = self.buf.at[k, p.z, p.h, p.l, :, self.cols(p.y)]
                local.append(pltpu.make_async_copy(s, d, self.send.at[self.index, 17]))
                for step in range(1, 8):
                    away.append(remote(s, d, self.send.at[self.index, 0], self.recv.at[self.index, 0],
                                       p.device(z=p.turn("z", step))))
        return local, away

    def first_size(self):
        p = self.place
        if self.kind == "z":
            return self.buf.at[:, p.z, p.h]
        return self.buf.at[:, pl.ds(0, 7), p.h, p.l, :, self.cols(p.y)]

    def copies(self, task):
        p = self.place
        if self.kind == "z":
            if task == 1:
                own = self.buf.at[:, p.z]
                return [(None, self.to(own, 1, z=p.turn("z", 1))), (None, self.to(own, 2, z=p.turn("z", -1))),
                        (None, self.to_core(own, 0))]
            if task == 5:
                far = p.turn("z", 4)
                return [((self.buf.at[:, far, 0], 7), None), ((self.buf.at[:, far, 1], 8), None),
                        (None, self.to_core(self.buf.at[:, far], 7))]
            found = []
            for n, sign in enumerate((1, -1)):
                c = p.turn("z", sign * (1 - task))
                slab = self.buf.at[:, c]
                onward = self.buf.at[:, c, n] if task == 4 else slab
                found.append(((slab, 2 * task - 3 + n), self.to(onward, 2 * task - 1 + n, z=p.turn("z", sign))))
                found.append((None, self.to_core(slab, 2 * task - 3 + n)))
            return found
        d1, d2 = self.kind[:2]
        if task == 1:
            own = self.part(1, getattr(p, d1))
            return [(None, self.to(own, 1, **{d1: p.turn(d1, 1)})), (None, self.to(own, 2, **{d1: p.turn(d1, -1)})),
                    (None, self.to(own, 3, **{d1: p.turn(d1, 2)}))]
        up, down, far = p.turn(d2, 1), p.turn(d2, -1), p.turn(d2, 2)
        low, high = pl.ds(0, 4), pl.ds(4, 4)
        direct = self.kind.endswith("u")
        if task == 2:
            own = self.part(2, getattr(p, d2))
            more = [(None, self.to(own, 7, **{d2: far}))] if direct else []
            return [((self.part(1, p.turn(d1, -1)), 1), None), ((self.part(1, p.turn(d1, 1)), 2), None),
                    ((self.part(1, p.turn(d1, 2)), 3), None),
                    (None, self.to(own, 5, **{d2: up})), (None, self.to(own, 6, **{d2: down})),
                    (None, self.to_core(own, 0))] + more
        if task == 3 and direct:
            return [((self.part(2, c), 5 + k), self.to_core(self.part(2, c), 1 + k))
                    for k, c in enumerate((down, up, far))]
        if task == 3:
            return [((self.part(2, down), 5), self.to(self.part(2, down, low), 7, **{d2: up})),
                    ((self.part(2, up), 6), self.to(self.part(2, up, high), 8, **{d2: down})),
                    (None, self.to_core(self.part(2, down), 1)), (None, self.to_core(self.part(2, up), 2))]
        return [((self.part(2, far, low), 7), None), ((self.part(2, far, high), 8), None),
                (None, self.to_core(self.part(2, far), 3))]

    def run(self, task):
        assert task == self.done, (self.chunk, task)
        self.done += 1

        @pl.when(self.place.core == self.core)
        def _():
            p = self.place
            if task == 0:
                local, away = self.first_copies()
                for copy in away + local:
                    copy.start()
                return
            if task == 1:
                own = self.buf.at[:, p.z, p.h]
                if self.kind != "z":
                    own = self.buf.at[:, p.z, p.h, p.l, :, self.cols(p.y)]
                wait_bytes(own, self.send.at[self.index, 17])
                wait_bytes(self.first_size(), self.recv.at[self.index, 0])
            for before, copy in self.copies(task):
                if before is not None:
                    wait_bytes(before[0], self.recv.at[self.index, before[1]])
                if copy is not None:
                    copy.start()

    def finish(self):
        @pl.when(self.place.core == self.core)
        def _():
            wait_bytes(self.first_size(), self.send.at[self.index, 0])
            for task in range(1, self.last + 1):
                for _, copy in self.copies(task):
                    if copy is not None:
                        copy.wait_send()

    def arrived(self):
        assert self.done == self.last + 1, self.chunk
        p = self.place

        @pl.when(p.core != self.core)
        def _():
            if self.kind == "z":
                refs = [self.buf.at[:, p.turn("z", n)] for n in (0, -1, 1, -2, 2, -3, 3, 4)]
            else:
                d2 = self.kind[1]
                refs = [self.part(2, p.turn(d2, n)) for n in (0, -1, 1, 2)]
            for k, ref in enumerate(refs):
                wait_bytes(ref, self.core_recv.at[self.index, k])


def normed(values, gain):
    centre = values - jnp.mean(values, axis=-1, keepdims=True)
    variance = jnp.mean(centre * centre, axis=-1, keepdims=True)
    return (centre * lax.rsqrt(variance + EPSILON) * gain).astype(BF16)


def dot(a, b):
    return jnp.dot(a, b, preferred_element_type=F32)


def dot_t(a, b):
    return lax.dot_general(a, b, (((1,), (1,)), ((), ())), preferred_element_type=F32)


def gelu(values):
    return (0.5 * values * (1.0 + lax.erf(values * (0.5 ** 0.5)))).astype(BF16)


def rounded(values):
    return values.astype(BF16).astype(F32)


def split(values):
    high = values.astype(BF16)
    return high, (values - high.astype(F32)).astype(BF16)


def lane_head(shape):
    return lax.div(lax.broadcasted_iota(jnp.int32, shape, len(shape) - 1), HD)


def head_rows(queries, count):
    own = lax.broadcasted_iota(jnp.int32, (HEADS, D), 0) == lane_head((HEADS, D))
    return jnp.concatenate([jnp.where(own, queries[n:n + 1], 0.0) for n in range(count)], axis=0)


def spread_matrix(rows, first):
    shape = (rows, D)
    own = lax.broadcasted_iota(jnp.int32, shape, 0) - first == lane_head(shape)
    return jnp.where(own, 1.0, 0.0).astype(BF16)


def score_matrix(queries, count, query_w, key_w, high_ref, low_ref):
    high, low = split(head_rows(dot(queries, query_w), count))
    high_ref[...], low_ref[...] = split(dot_t(key_w, high) + dot_t(key_w, low))


def rows_of(index, size):
    return pl.ds(pl.multiple_of(index * size, size & -size), size)


def norm_rows(load, dst, gain, rows, block=48):
    def step(n, _):
        dst[rows_of(n, block)] = normed(load(rows_of(n, block)), gain)
        return 0
    lax.fori_loop(0, rows // block, step, 0, unroll=True)


def attention(packed, attended, mask, w):
    lane = lane_head((WINDOW, 128))
    ones = jnp.ones((WINDOW, 128), BF16)
    rows = slice(WINDOW * w, WINDOW * w + WINDOW)
    for g in range(4):
        q, k, v = (packed[rows, 128 * g + part * D:128 * g + part * D + 128] for part in range(3))
        both = jnp.concatenate([v, ones], axis=1)
        total = jnp.zeros((WINDOW, 128), F32)
        for m in range(4):
            e = jnp.exp(dot_t(jnp.where(lane == m, q, jnp.zeros_like(q)), k) * SCALE)
            if mask is not None:
                e = e * mask
            mixed = dot(e.astype(BF16), both)
            total = jnp.where(lane == m, mixed[:, :128] / mixed[:, 128:], total)
        attended[rows, 128 * g:128 * g + 128] = total.astype(BF16)


def kernel(plan, *refs):
    (latents_ref, codes_ref, gains_ref, regions_ref), refs = refs[:4], refs[4:]
    sources, refs = dict(zip(WEIGHTS, refs[:12])), refs[12:]
    far, refs = refs[:8], refs[8:]
    out_ref, refs = refs[0], refs[1:]
    near, refs = refs[:8], refs[8:]
    levels_ref, surface_ref, pack1a, pack1b, open1, pack2a, pack2b, open2 = near
    buffers, refs = refs[:len(CHUNKS)], refs[len(CHUNKS):]
    (send, recv, core_recv, halo_send, halo_recv, tiled, norm, values, expo, fa_high, fa_low, fd_high, fd_low,
     grid, packed, attended, grid_norm, total, hidden, masks, out1, in1, out2, in2, dec_expo, result,
     near_sem, out_sem) = refs

    place = Place()
    loads = [pltpu.make_async_copy(src, dst, near_sem.at[n]) for n, (src, dst) in enumerate(zip(far, near))]
    for load in loads:
        load.start()
    barrier = pltpu.get_barrier_semaphore()
    friends = [place.device(z=place.turn("z", n)) for n in range(1, 8)]
    friends += [place.device(x=place.turn("x", n)) for n in range(1, 4)]
    friends += [place.device(y=place.turn("y", n)) for n in range(1, 4)]
    friends += [place.device(core=1 - place.core)]
    friends += [place.beside(i, j) for i, j in ((1, 0), (0, 1), (1, 1), (-1, 0), (0, -1), (-1, -1))]
    for friend in friends:
        pl.semaphore_signal(barrier, inc=1, device_id=friend, device_id_type=pl.DeviceIdType.MESH)
    pl.semaphore_wait(barrier, len(friends))
    carriers, count = [], [0, 0]
    for chunk, buf in zip(CHUNKS, buffers):
        own = [sources[w] if k is None else sources[w].at[k] for w, k in chunk[0]]
        carriers.append(Carrier(place, chunk, own, buf, count[chunk[3]], send, recv, core_recv))
        count[chunk[3]] += 1
    pairs = list(zip(carriers[0::2], carriers[1::2]))

    def pump(point):
        for pair, task in plan.get(point, ()):
            for carrier in pairs[pair]:
                carrier.run(task)

    def weight(n, k=0):
        buf = buffers[n]
        return buf[k].reshape(16 * CHUNKS[n][1], CHUNKS[n][2])

    def ready(*numbers):
        for n in numbers:
            carriers[n].arrived()

    pump("start")
    tiled[:, 936:960] = jnp.zeros((4, 24, 128), F32)
    loads[0].wait()
    loads[1].wait()
    for n in range(PATCHES):
        rows = levels_ref[n // 12, n % 12].astype(F32)
        for c in range(4):
            tiled[c, pl.ds(n, LEVELS, stride=PATCHES)] = rows[:, 128 * c:128 * c + 128]
    for i in range(6):
        grid[12 * i:12 * i + 12] = surface_ref[i].astype(F32)
    pump("compact")
    norm_rows(lambda rows: jnp.concatenate([tiled[c, rows] for c in range(4)], axis=1), norm, gains_ref[0:1], ROWS)
    pump("norm")
    ready(0)
    score_matrix(latents_ref[...], LATENT, weight(0, 0), weight(0, 1), fa_high, fa_low)
    pump("agg_matrix")

    def score_step(n, _):
        block = norm[rows_of(n, 192)]
        expo[rows_of(n, 192)] = jnp.exp((dot(block, fa_high[...]) + dot(block, fa_low[...])) * SCALE)
        return 0
    lax.fori_loop(0, ROWS // 192, score_step, 0)
    pump("agg_scores")
    ready(1)

    def value_step(n, _):
        values[rows_of(n, 192)] = dot(norm[rows_of(n, 192)], weight(1, 0))
        return 0
    lax.fori_loop(0, ROWS // 192, value_step, 0)
    pump("agg_values")
    level_rows = [slice(PATCHES * n, PATCHES * n + PATCHES) for n in range(LEVELS)]
    inverse = 1.0 / sum(expo[rows] for rows in level_rows)
    probs = jnp.concatenate([expo[rows] * inverse for rows in level_rows], axis=0).astype(BF16)
    for a in range(LATENT):
        spread = spread_matrix(LATENT * HEADS, HEADS * a)
        for cols in (slice(0, 256), slice(256, 512)):
            wide = dot(probs, spread[:, cols])
            total[PATCHES * a:PATCHES * a + PATCHES, cols] = sum(wide[rows] * values[rows, cols] for rows in level_rows)
        pump("agg_mix%d" % a)
    projected = dot(total[0:216].astype(BF16), weight(1, 1))
    for a in range(LATENT):
        rows = projected[PATCHES * a:PATCHES * a + PATCHES]
        grid[PATCHES * (a + 1):PATCHES * (a + 2)] = rounded(latents_ref[a:a + 1].astype(F32) + rows)
    pump("agg_out")

    def block(b, done):
        name = "b%d_" % b
        norm_rows(lambda rows: grid[rows], grid_norm, gains_ref[2 + 2 * b:3 + 2 * b], TOKENS)
        qkv_n, proj_n = (7, 6) if b else (2, 3)
        in_n, out_n = (8, 9) if b else (4, 5)
        ready(qkv_n)
        for n in range(6):
            cols = buffers[qkv_n][0, :, :, :, :, 256 * n:256 * n + 256].reshape(D, 256)
            packed[:, 256 * n:256 * n + 256] = dot(grid_norm[...], cols).astype(BF16)
        pump(name + "qkv")
        for w in range(2):
            attention(packed, attended, masks[w] if b else None, w)
            pump(name + "attention%d" % w)
        ready(proj_n)
        grid[...] = rounded(grid[...] + dot(attended[...], weight(proj_n)))
        pump(name + "proj")
        norm_rows(lambda rows: grid[rows], grid_norm, gains_ref[3 + 2 * b:4 + 2 * b], TOKENS)
        ready(in_n)
        for part in range(4):
            cols = slice(512 * part, 512 * part + 512)
            hidden[:, cols] = gelu(dot_t(grid_norm[...], buffers[in_n][0, 2 * part:2 * part + 2].reshape(512, D)))
            pump(name + "mlp%d" % part)
        ready(out_n)
        for w in range(2):
            rows = slice(WINDOW * w, WINDOW * w + WINDOW)
            total[rows] = grid[rows] + dot(hidden[rows], weight(out_n))
            done(w)
            pump(name + "half%d" % w)

    def exchange(source, target, first, size, slot, own, sends):
        at = [pl.ds(first + q * size, size) for q in range(4)]
        copies = [remote(source.at[at[q]], target.at[at[q]], halo_send.at[slot, n], halo_recv.at[slot, n],
                         place.beside(i, j)) for n, (q, i, j) in enumerate(sends)]
        copies.append(pltpu.make_async_copy(source.at[at[own]], target.at[at[own]], halo_send.at[slot, 3]))
        for copy in copies:
            copy.start()
        moving.extend(copies)

    moving = []
    for load in loads[2:]:
        load.wait()

    def first_half_windows(w):
        rows = slice(WINDOW * w, WINDOW * w + WINDOW)
        out1[192 * w:192 * w + 192] = dot((pack1a, pack1b)[w][...], total[rows].astype(BF16)).astype(BF16)
        exchange(out1, in1, 192 * w, 48, w, 3, ((0, -1, -1), (1, -1, 0), (2, 0, -1)))

    def last_half_windows(w):
        size, rows = (48, 32)[w], slice(WINDOW * w, WINDOW * w + WINDOW)
        out2[192 * w:192 * w + 4 * size] = dot((pack2a, pack2b)[w][...], total[rows].astype(BF16)).astype(BF16)
        exchange(out2, in2, 192 * w, size, 2 + w, 0, ((3, 1, 1), (2, 1, 0), (1, 0, 1)))

    def arrive():
        while moving:
            moving.pop(0).wait()

    block(0, first_half_windows)
    pump("halo1")
    ids = [[regions_ref[level, i] for i in range(6)] for level in range(4)]
    for w in range(2):
        rows_id = jnp.zeros((WINDOW, WINDOW), jnp.int32)
        cols_id = jnp.zeros((WINDOW, WINDOW), jnp.int32)
        for n in range(12):
            value = ids[2 * w + n // 6][n % 6]
            rows_id = jnp.where(lax.broadcasted_iota(jnp.int32, (WINDOW, WINDOW), 0) >= 12 * n, value, rows_id)
            cols_id = jnp.where(lax.broadcasted_iota(jnp.int32, (WINDOW, WINDOW), 1) >= 12 * n, value, cols_id)
        masks[w] = jnp.where(rows_id == cols_id, 1.0, 0.0)
    arrive()
    grid[...] = dot(open1[...], in1[...])
    block(1, last_half_windows)
    pump("halo2")
    ready(10)
    score_matrix(codes_ref[...], LEVELS, weight(10, 0), weight(10, 1), fd_high, fd_low)
    arrive()
    atmos = normed(dot(open2[...], in2[...]), gains_ref[1:2])
    expos = jnp.exp((dot(atmos, fd_high[...]) + dot(atmos, fd_low[...])) * SCALE)
    inverse = 1.0 / (expos[:PATCHES] + expos[PATCHES:2 * PATCHES] + expos[2 * PATCHES:])
    dec_expo[...] = expos * jnp.concatenate([inverse] * LATENT, axis=0)
    ready(11)
    total[0:216] = dot(atmos, weight(11, 0))

    spread = spread_matrix(HEADS, 0)
    for n in range(LEVELS):
        wide = dot(dec_expo[:, HEADS * n:HEADS * n + HEADS].astype(BF16), spread) * total[0:216]
        values[PATCHES * n:PATCHES * n + PATCHES] = (
            wide[:PATCHES] + wide[PATCHES:2 * PATCHES] + wide[2 * PATCHES:])

    def out_step(n, _):
        rows = dot(values[rows_of(n, 192)].astype(BF16), weight(11, 1))
        for c in range(4):
            tiled[c, rows_of(n, 192)] = rows[:, 128 * c:128 * c + 128]
        return 0
    lax.fori_loop(0, ROWS // 192, out_step, 0)
    codes = codes_ref[...].astype(F32)
    stores = [pltpu.make_async_copy(result.at[i], out_ref.at[i], out_sem.at[i]) for i in range(6)]
    for n in range(PATCHES):
        rows = jnp.concatenate([tiled[c, pl.ds(n, LEVELS, stride=PATCHES)] for c in range(4)], axis=1)
        result[n // 12, n % 12] = (codes + rows).astype(BF16)
        if n % 12 == 11:
            stores[n // 12].start()
    for store in stores:
        store.wait()
    for carrier in carriers:
        carrier.finish()


def one_hot(targets, sources):
    return (np.asarray(targets)[:, None] == np.arange(sources)[None, :]).astype(np.float32)


def permutations():
    def quarter(q, z, i, j):
        return (z * 6 + 3 * (q // 2) + i) * 12 + 6 * (q % 2) + j

    def pack(levels, size):
        picked = []
        for q in range(4):
            rows = [quarter(q, z, i, j) for z in range(levels) for i in range(3) for j in range(6)]
            picked += rows + [-1] * (size - len(rows))
        return one_hot(picked, WINDOW)

    open_a, open_b = [], []
    for z in range(4):
        for i in range(6):
            for j in range(12):
                q, at = 2 * (1 - i // 3) + (1 - j // 6), i % 3 * 6 + j % 6
                level = (z + 1) % 4
                open_a.append(192 * (level // 2) + 48 * q + 18 * (level % 2) + at)
                if z > 0:
                    open_b.append(192 + 32 * q + at if z == 3 else 48 * q + 18 * (z - 1) + at)
    return pack(2, 48), pack(2, 48), one_hot(open_a, 384), pack(2, 48), pack(1, 32), one_hot(open_b, 320)


PLAN = {
    "start": ((0, 0), (3, 0), (1, 0), (2, 0), (2, 1), (0, 1), (3, 1), (1, 1), (0, 2), (4, 0), (5, 0), (2, 2), (1, 2), (4, 1),),
    "compact": ((0, 3),),
    "norm": ((3, 2), (2, 3), (1, 3), (4, 2),),
    "agg_mix0": ((2, 4), (3, 3),),
    "agg_mix2": ((1, 4),),
    "agg_out": ((5, 1),),
    "b0_attention1": ((2, 5), (4, 3),),
    "halo1": ((5, 2), (3, 4), (4, 4),),
    "b1_attention1": ((5, 3),),
    "halo2": ((5, 4),),
}


def body(levels_in, surface, latents, level_codes, norm_gains, agg_query_w, agg_key_w, agg_value_w, agg_out_w,
         dec_query_w, dec_key_w, dec_value_w, dec_out_w, qkv_w, proj_w, mlp_in, mlp_out, regions):
    named = dict(agg_query_w=agg_query_w, agg_key_w=agg_key_w, agg_value_w=agg_value_w, agg_out_w=agg_out_w,
                 dec_query_w=dec_query_w, dec_key_w=dec_key_w, dec_value_w=dec_value_w, dec_out_w=dec_out_w,
                 qkv_w=qkv_w, proj_w=proj_w, mlp_in=mlp_in, mlp_out=mlp_out)
    vmem, smem = pl.BlockSpec(memory_space=pltpu.VMEM), pl.BlockSpec(memory_space=pltpu.SMEM)
    far = pl.BlockSpec(memory_space=pl.ANY)
    loaded = [jnp.transpose(levels_in, (1, 2, 0, 3)), surface] + [jnp.asarray(m, BF16) for m in permutations()]
    decoded = pl.pallas_call(
        functools.partial(kernel, PLAN),
        out_shape=jax.ShapeDtypeStruct((6, 12, LEVELS, D), BF16),
        in_specs=[vmem] * 3 + [smem] + [far] * 20,
        out_specs=far,
        scratch_shapes=[pltpu.VMEM(a.shape, BF16) for a in loaded] + [
            pltpu.VMEM(buffer_shape(chunk), BF16) for chunk in CHUNKS] + [
            pltpu.SemaphoreType.DMA((6, 18)),
            pltpu.SemaphoreType.DMA((6, 9)),
            pltpu.SemaphoreType.DMA((6, 8)),
            pltpu.SemaphoreType.DMA((4, 4)),
            pltpu.SemaphoreType.DMA((4, 3)),
            pltpu.VMEM((4, ROWS, 128), F32),
            pltpu.VMEM((ROWS, D), BF16),
            pltpu.VMEM((ROWS, D), F32),
            pltpu.VMEM((ROWS, LATENT * HEADS), F32),
            pltpu.VMEM((D, LATENT * HEADS), BF16),
            pltpu.VMEM((D, LATENT * HEADS), BF16),
            pltpu.VMEM((D, LEVELS * HEADS), BF16),
            pltpu.VMEM((D, LEVELS * HEADS), BF16),
            pltpu.VMEM((TOKENS, D), F32),
            pltpu.VMEM((TOKENS, 3 * D), BF16),
            pltpu.VMEM((TOKENS, D), BF16),
            pltpu.VMEM((TOKENS, D), BF16),
            pltpu.VMEM((TOKENS, D), F32),
            pltpu.VMEM((TOKENS, 4 * D), BF16),
            pltpu.VMEM((2, WINDOW, WINDOW), F32),
            pltpu.VMEM((384, D), BF16),
            pltpu.VMEM((384, D), BF16),
            pltpu.VMEM((320, D), BF16),
            pltpu.VMEM((320, D), BF16),
            pltpu.VMEM((216, LEVELS * HEADS), F32),
            pltpu.VMEM((6, 12, LEVELS, D), BF16),
            pltpu.SemaphoreType.DMA((8,)),
            pltpu.SemaphoreType.DMA((6,)),
        ],
        compiler_params=pltpu.CompilerParams(collective_id=0, has_side_effects=True, vmem_limit_bytes=58 * 2 ** 20),
        cost_estimate=pl.CostEstimate(flops=7 * 10 ** 9, bytes_accessed=10 ** 7, transcendentals=10 ** 7),
    )(latents, level_codes, norm_gains, regions, *[named[w] for w in WEIGHTS], *loaded)
    return jnp.transpose(decoded, (2, 0, 1, 3))


def solution(mesh):
    split_rows, split_middle = P("lat", None), P(None, "lat", None)
    in_specs = (P(None, "lat", "lon", None), P("lat", "lon", None), P(), P(), P()) + (split_rows,) * 8 + (
        split_middle,) * 4 + (P(None, "lat"),)
    return jax.shard_map(body, mesh=mesh, in_specs=in_specs, out_specs=P(None, "lat", "lon", None), check_vma=False)
```
